256 devices in a mesh: ex: 16 (over z_lo, x, core), mod: 16 (over z_hi, y).
Axes of the slice: x: 4, y: 4, z: 8 (z_hi: 4, z_lo: 2; z = z_hi * 2 + z_lo), core: 2. Of those that a mesh axis runs over, the one named last changes fastest.
Arguments:
- train_grads: bfloat16 [128, 16384, 256], P('mod', 'ex'), may hold values from -6 to 6
- test_grads: bfloat16 [128, 2048, 256], P('mod', 'ex'), may hold values from -0.046875 to 0.046875
- left_inv: float32 [128, 16, 16], P('mod'), may hold values from -1 to 3, as said below
- right_inv: float32 [128, 16, 16], P('mod'), may hold values from -1 to 3, as said below
Outputs:
- scores: float32 [2048, 16384], P('mod', 'ex')
The draws below stay inside these ranges and needn't reach their ends.
Inputs may be any that keep to these rules, and one draw needn't show every extreme that they name: `left_inv`: each module's matrix has a positive diagonal. `right_inv`: each module's matrix has a positive diagonal.
All inputs are finite; a program needn't handle non-finite values.
Results may differ from the reference program's by a relative error of at most 0.0029.
Values may be sent and summed in bfloat16 or wider, within the bound.
No kernel may reach another device: no remote copies, remote signals or barrier semaphores. Data moves between devices by JAX's collectives and lax.ppermute only.
A program may use at most 128 MiB of HBM per device.

```python
import jax
import jax.numpy as jnp
from jax import lax

FACTOR = 16
R = 256
MODULES = 128
NTRAIN = 16384
NTEST = 2048


def factor_draw(rng_key, module_count, factor_width, low_end, high_end, spread):
    first_key, second_key = jax.random.split(rng_key)
    diagonal = jax.random.uniform(first_key, (module_count, factor_width), jnp.float32, low_end, high_end)
    off_diagonal = spread * jnp.clip(jax.random.normal(second_key, (module_count, factor_width, factor_width), jnp.float32), -3.0, 3.0)
    identity = jnp.eye(factor_width, dtype=jnp.float32)
    return off_diagonal * (1.0 - identity) + identity * diagonal[:, :, None]


def draw_left_inv(key, part):
    key = jax.random.fold_in(key, 11)
    return factor_draw(key, MODULES, FACTOR, 1.0, 2.0, 0.1)


def draw_right_inv(key, part):
    key = jax.random.fold_in(key, 23)
    return factor_draw(key, MODULES, FACTOR, 1.0, 2.0, 0.1)


def raised(drawn, own_key, source, target, shards_of, factor):
    owner, partner = [(jnp.arange(drawn.shape[axis_at]) // (drawn.shape[axis_at] // shards_of)).reshape([-1 if axis == axis_at else 1 for axis in range(drawn.ndim)]) for axis_at in (source, target)]
    chosen = jax.random.permutation(own_key, shards_of)[partner]
    strong = (owner == chosen) | (owner == (partner + shards_of // 2) % shards_of)
    return jnp.where(strong, factor * drawn, drawn)


def level_of(stream_key, shape, shards, least, top_value):
    level, own = 1.0, jax.random.fold_in(stream_key, 6)
    for axis_at, parts in shards:
        heights = jnp.exp(jax.random.uniform(jax.random.fold_in(own, axis_at), (parts,), jnp.float32, least / len(shards), top_value / len(shards)))
        level = level * jnp.repeat(heights, shape[axis_at] // parts).reshape([-1 if axis == axis_at else 1 for axis in range(len(shape))])
    return level


def bell_draw(key, shape, scale, most, cuts=(), held_as=jnp.bfloat16):
    entries = jax.random.normal(key, shape, jnp.float32) * scale
    if len(cuts) > 0:
        entries = level_of(key, shape, cuts, -0.22, 0.18) * entries
    return jnp.clip(entries, min=-most, max=most).astype(held_as)


def noise_with(own_key, shape, deviation, bound, cuts, heavy, kind=jnp.bfloat16):
    result = deviation * jax.random.normal(own_key, shape, jnp.float32)
    if cuts:
        result = result * level_of(own_key, shape, cuts, -0.22, 0.18)
    return jnp.clip(raised(result, jax.random.fold_in(own_key, 3), *heavy), -bound, bound).astype(kind)


def setup_inputs(seed: int = 0) -> dict:
    streams_of = jax.random.split(jax.random.key(seed), 5)
    train_grads = bell_draw(streams_of[0], (MODULES, NTRAIN, R), 1.0, 6.0, ((0, 16), (1, 16)))
    test_grads = noise_with(streams_of[1], (MODULES, NTEST, R), (MODULES * R) ** -0.5, 0.046875, ((0, 16), (1, 16)), (0, 1, 16, 2.0))
    left_inv = draw_left_inv(jax.random.fold_in(streams_of[4], 71), 0)
    right_inv = draw_right_inv(jax.random.fold_in(streams_of[4], 71), 0)
    return {"train_grads": train_grads, "test_grads": test_grads, "left_inv": left_inv, "right_inv": right_inv}


def precondition(grads, left_inv, right_inv):
    module_count = grads.shape[0]
    row_count = grads.shape[1]
    factor_width = left_inv.shape[1]
    matrices = grads.astype(jnp.float32).reshape(module_count, row_count, factor_width, factor_width)
    halfway = jnp.einsum("mac,mecd->mead", left_inv, matrices, precision=lax.Precision.HIGHEST)
    mapped = jnp.einsum("mead,mdb->meab", halfway, right_inv, precision=lax.Precision.HIGHEST)
    return mapped.reshape(module_count, row_count, factor_width * factor_width).astype(jnp.bfloat16)


def reference(train_grads, test_grads, left_inv, right_inv):
    features = precondition(test_grads, left_inv, right_inv)

    def module_step(running, blocks_pair):
        feature_block, train_block = blocks_pair
        added = lax.dot_general(feature_block, train_block, (((1,), (1,)), ((), ())), preferred_element_type=jnp.float32)
        return running + added, None

    initial = jnp.zeros((features.shape[1], train_grads.shape[1]), jnp.float32)
    scores, unused = lax.scan(module_step, initial, (features, train_grads))
    return scores
```

```python
import functools

import jax
import jax.numpy as jnp
from jax import lax
from jax.experimental import pallas as pl
from jax.experimental.pallas import tpu as pltpu
from jax.sharding import PartitionSpec as P

F32 = jnp.float32
BF16 = jnp.bfloat16
CHUNKS = (64, 64)
VMEM_LIMIT = 48 * 1024 * 1024


def ex_perm(move):
    pairs = []
    for i in range(16):
        z, x, c = i // 8, (i // 2) % 4, i % 2
        z, x, c = move(z, x, c)
        pairs.append((i, ((z % 2) * 4 + x % 4) * 2 + c % 2))
    return pairs


def mod_perm(move):
    pairs = []
    for i in range(16):
        h, y = move(i // 4, i % 4)
        pairs.append((i, (h % 4) * 4 + y % 4))
    return pairs


def to_x(d):
    return ex_perm(lambda z, x, c: (z, x + d, c))


TO_Z = ex_perm(lambda z, x, c: (z + 1, x, c))
TO_CORE = ex_perm(lambda z, x, c: (z, x, c + 1))


def to_y(d):
    return mod_perm(lambda h, y: (h, y + d))


def to_h(d):
    return mod_perm(lambda h, y: (h + d, y))


def call(kernel, out_shape, in_specs, out_specs, scratch, flops, moved, name):
    return pl.pallas_call(
        kernel,
        out_shape=out_shape,
        in_specs=in_specs,
        out_specs=out_specs,
        scratch_shapes=scratch,
        compiler_params=pltpu.CompilerParams(vmem_limit_bytes=VMEM_LIMIT),
        cost_estimate=pl.CostEstimate(flops=flops, bytes_accessed=moved, transcendentals=0),
        name=name,
    )


VM = pl.BlockSpec(memory_space=pltpu.VMEM)
SM = pl.BlockSpec(memory_space=pltpu.SMEM)
ANY = pl.BlockSpec(memory_space=pl.ANY)


def kron_kernel(left_ref, right_ref, w_ref):
    width = left_ref.shape[1]
    full = width * width
    wide = lax.broadcasted_iota(jnp.int32, (width, full), 1)
    narrow = lax.broadcasted_iota(jnp.int32, (width, full), 0)
    outer = jnp.where(wide // width == narrow, 1.0, 0.0).astype(F32)
    inner = jnp.where(wide % width == narrow, 1.0, 0.0).astype(F32)
    dot = functools.partial(
        lax.dot_general, precision=lax.Precision.HIGHEST, preferred_element_type=F32
    )
    for m in range(left_ref.shape[0]):
        l1 = dot(left_ref[m], outer, (((0,), (0,)), ((), ())))
        lx = dot(outer, l1, (((0,), (0,)), ((), ())))
        r1 = dot(right_ref[m], inner, (((1,), (0,)), ((), ())))
        rx = dot(inner, r1, (((0,), (0,)), ((), ())))
        w = lx * rx
        hi = w.astype(BF16)
        rest = w - hi.astype(F32)
        mid = rest.astype(BF16)
        w_ref[m, 0] = hi
        w_ref[m, 1] = mid
        w_ref[m, 2] = (rest - mid.astype(F32)).astype(BF16)


def make_kron(left, right):
    m, n, _ = left.shape
    return call(
        kron_kernel,
        jax.ShapeDtypeStruct((m, 3, n * n, n * n), BF16),
        [VM, VM], VM, [], 4 * 10**8, 4 * 10**6, "kron",
    )(left, right)


def features_kernel(places, ids, *refs):
    pieces, (w_ref, out_ref) = refs[: len(places)], refs[len(places):]
    z, x = ids[0], ids[1]
    modules, rows, width = pieces[0].shape
    slots = [
        lax.rem(z + dz, 2) * 4 + lax.rem(x + dx, 4) for dz, dx in places
    ]
    for m in range(modules):
        g = jnp.concatenate([p[m] for p in pieces], axis=0)
        f = jnp.dot(g, w_ref[m, 2], preferred_element_type=F32)
        f += jnp.dot(g, w_ref[m, 1], preferred_element_type=F32)
        f += jnp.dot(g, w_ref[m, 0], preferred_element_type=F32)
        f = f.astype(BF16)
        for k, slot in enumerate(slots):
            out_ref[slot, :, m * width:(m + 1) * width] = f[k * rows:(k + 1) * rows]


def make_features(ids, pieces, w):
    places = tuple(pieces)
    arrays = [pieces[p] for p in places]
    modules, rows, width = arrays[0].shape
    n = len(places)
    return call(
        functools.partial(features_kernel, places),
        jax.ShapeDtypeStruct((n, rows, modules * width), BF16),
        [SM] + [VM] * n + [VM], VM, [],
        6 * n * rows * modules * width * width, 3 * n * rows * modules * width, "features",
    )(ids, *arrays, w)


def product_kernel(shifts, finish, n_extra, n_out, ids, mine, other, train, *refs):
    extra, outs = refs[:n_extra], refs[n_extra:n_extra + n_out]
    t_buf, f_buf, acc, t_sem, f_sem = refs[n_extra + n_out:]
    core, y = ids[2], ids[3]
    modules = train.shape[0]
    rows = mine.shape[1]
    width = train.shape[2]

    def copies(k, source):
        part = lax.rem(y + shifts[k], 4) // 2
        return [
            pltpu.make_async_copy(source.at[2 * h + part], f_buf.at[k, h], f_sem.at[k, h])
            for h in range(4)
        ]

    for k, shift in enumerate(shifts):
        owner = lax.rem(y + shift, 2)

        @pl.when(owner == core)
        def _():
            for cp in copies(k, mine):
                cp.start()

        @pl.when(owner != core)
        def _():
            for cp in copies(k, other):
                cp.start()

    for m in range(modules):
        pltpu.make_async_copy(train.at[m], t_buf.at[m], t_sem.at[m]).start()
    for k in range(len(shifts)):
        for cp in copies(k, mine):
            cp.wait()
    n = len(shifts) * 4 * rows

    for m in range(modules):
        pltpu.make_async_copy(train.at[m], t_buf.at[m], t_sem.at[m]).wait()
        f = f_buf[:, :, :, m * width:(m + 1) * width].reshape(n, width)
        part = lax.dot_general(
            f, t_buf[m], (((1,), (1,)), ((), ())), preferred_element_type=F32
        )
        if m == 0:
            acc[...] = part
        else:
            acc[...] += part
    finish(ids, acc, extra, outs)


def product(shifts, finish, out_shape, ids, mine, other, train, extra, name):
    rows = mine.shape[1]
    depth = mine.shape[2]
    modules, columns, width = train.shape
    n = len(shifts) * 4 * rows
    return call(
        functools.partial(product_kernel, shifts, finish, len(extra), len(out_shape)),
        out_shape,
        [SM, ANY, ANY, ANY] + [VM] * len(extra),
        [VM] * len(out_shape),
        [
            pltpu.VMEM(train.shape, BF16),
            pltpu.VMEM((len(shifts), 4, rows, depth), BF16),
            pltpu.VMEM((n, columns), F32),
            pltpu.SemaphoreType.DMA((modules,)),
            pltpu.SemaphoreType.DMA((len(shifts), 4)),
        ],
        2 * n * depth * columns, 2 * (n * depth + depth * columns + n * columns), name,
    )(ids, mine, other, train, *extra)


def finish_far(ids, acc, extra, outs):
    rows = outs[0].shape[1]
    for h in range(4):
        outs[h // 2][h % 2] = acc[h * rows:(h + 1) * rows].astype(BF16)


def finish_near(ids, acc, extra, outs):
    rows = outs[0].shape[1]
    for k in range(2):
        for h in range(4):
            at = (k * 4 + h) * rows
            part = acc[at:at + rows]
            if h // 2 == k:
                part = part + extra[k][h % 2].astype(F32)
            outs[k][h] = part.astype(BF16)


def finish_own(ids, acc, extra, outs):
    hi = ids[4]
    rows = outs[0].shape[0]
    for k in range(4):
        h = lax.rem(hi + k, 4)
        total = acc[pl.ds(pl.multiple_of(h * rows, rows), rows), :]
        for e in extra:
            total = total + e[h].astype(F32)
        outs[k][...] = total.astype(outs[k].dtype)


def total_kernel(*refs):
    out = refs[-1]
    at = 0
    for k in range(0, len(refs) - 1, 4):
        rows = refs[k].shape[0]
        total = refs[k][...]
        for r in refs[k + 1:k + 4]:
            total = total + r[...].astype(F32)
        out[at:at + rows] = total
        at += rows


def gather_pieces(own):
    send = functools.partial(lax.ppermute, axis_name="ex")
    z = send(own, perm=TO_Z)
    left = send(own, perm=to_x(1))
    right = send(own, perm=to_x(-1))
    far = send(own, perm=to_x(2))
    z_left = send(z, perm=to_x(1))
    z_right = send(z, perm=to_x(-1))
    z_far = send(far, perm=TO_Z)
    return {
        (0, 0): own, (1, 0): z, (0, 3): left, (0, 1): right, (0, 2): far,
        (1, 3): z_left, (1, 1): z_right, (1, 2): z_far,
    }


def body(train_grads, test_grads, left_inv, right_inv):
    ex = lax.axis_index("ex")
    mod = lax.axis_index("mod")
    ids = jnp.stack([ex // 8, (ex // 2) % 4, ex % 2, mod % 4, mod // 4]).astype(jnp.int32)
    columns = train_grads.shape[1]
    w = make_kron(left_inv, right_inv)
    at = 0
    parts = []
    for rows in CHUNKS:
        pieces = gather_pieces(test_grads[:, at:at + rows])
        at += rows
        mine = make_features(ids, pieces, w)
        other = lax.ppermute(mine, "ex", TO_CORE)
        half = jax.ShapeDtypeStruct((2, rows, columns), BF16)
        whole = jax.ShapeDtypeStruct((4, rows, columns), BF16)
        one = jax.ShapeDtypeStruct((rows, columns), BF16)
        keep = jax.ShapeDtypeStruct((rows, columns), F32)
        up, down = product((2,), finish_far, [half] * 2, ids, mine, other, train_grads, [], "far")
        up = lax.ppermute(up, "mod", to_y(1))
        down = lax.ppermute(down, "mod", to_y(-1))
        up, down = product(
            (1, 3), finish_near, [whole] * 2, ids, mine, other, train_grads, [up, down], "near"
        )
        up = lax.ppermute(up, "mod", to_y(1))
        down = lax.ppermute(down, "mod", to_y(-1))
        own, h1, h2, h3 = product(
            (0,), finish_own, [keep] + [one] * 3, ids, mine, other, train_grads, [up, down], "own"
        )
        parts += [
            own,
            lax.ppermute(h1, "mod", to_h(1)),
            lax.ppermute(h2, "mod", to_h(2)),
            lax.ppermute(h3, "mod", to_h(3)),
        ]
    rows = test_grads.shape[1]
    return call(
        total_kernel,
        jax.ShapeDtypeStruct((rows, columns), F32),
        [VM] * len(parts), VM, [],
        4 * rows * columns, 16 * rows * columns, "total",
    )(*parts)


def solution(mesh):
    return jax.shard_map(
        body,
        mesh=mesh,
        in_specs=(
            P("mod", "ex", None),
            P("mod", "ex", None),
            P("mod", None, None),
            P("mod", None, None),
        ),
        out_specs=P("mod", "ex"),
        check_vma=False,
    )
```

```python
import functools

import jax
import jax.numpy as jnp
from jax import lax
from jax.experimental import pallas as pl
from jax.experimental.pallas import tpu as pltpu
from jax.sharding import PartitionSpec as P

F32 = jnp.float32
BF16 = jnp.bfloat16
CHUNKS = (64, 64)
VMEM_LIMIT = 20 * 1024 * 1024


def ex_perm(move):
    pairs = []
    for i in range(16):
        z, x, c = i // 8, (i // 2) % 4, i % 2
        z, x, c = move(z, x, c)
        pairs.append((i, ((z % 2) * 4 + x % 4) * 2 + c % 2))
    return pairs


def mod_perm(move):
    pairs = []
    for i in range(16):
        h, y = move(i // 4, i % 4)
        pairs.append((i, (h % 4) * 4 + y % 4))
    return pairs


def to_x(d):
    return ex_perm(lambda z, x, c: (z, x + d, c))


TO_Z = ex_perm(lambda z, x, c: (z + 1, x, c))
TO_CORE = ex_perm(lambda z, x, c: (z, x, c + 1))


def to_y(d):
    return mod_perm(lambda h, y: (h, y + d))


def to_h(d):
    return mod_perm(lambda h, y: (h + d, y))


def call(kernel, out_shape, in_specs, out_specs, scratch, flops, moved, name):
    return pl.pallas_call(
        kernel,
        out_shape=out_shape,
        in_specs=in_specs,
        out_specs=out_specs,
        scratch_shapes=scratch,
        compiler_params=pltpu.CompilerParams(vmem_limit_bytes=VMEM_LIMIT),
        cost_estimate=pl.CostEstimate(flops=flops, bytes_accessed=moved, transcendentals=0),
        name=name,
    )


VM = pl.BlockSpec(memory_space=pltpu.VMEM)
SM = pl.BlockSpec(memory_space=pltpu.SMEM)
ANY = pl.BlockSpec(memory_space=pl.ANY)


def kron_kernel(left_ref, right_ref, w_ref):
    width = left_ref.shape[1]
    full = width * width
    wide = lax.broadcasted_iota(jnp.int32, (width, full), 1)
    narrow = lax.broadcasted_iota(jnp.int32, (width, full), 0)
    outer = jnp.where(wide // width == narrow, 1.0, 0.0).astype(F32)
    inner = jnp.where(wide % width == narrow, 1.0, 0.0).astype(F32)
    dot = functools.partial(
        lax.dot_general, precision=lax.Precision.HIGHEST, preferred_element_type=F32
    )
    for m in range(left_ref.shape[0]):
        l1 = dot(left_ref[m], outer, (((0,), (0,)), ((), ())))
        lx = dot(outer, l1, (((0,), (0,)), ((), ())))
        r1 = dot(right_ref[m], inner, (((1,), (0,)), ((), ())))
        rx = dot(inner, r1, (((0,), (0,)), ((), ())))
        w = lx * rx
        high = w.astype(BF16)
        w_ref[m, :full] = high
        w_ref[m, full:] = (w - high.astype(F32)).astype(BF16)


def make_kron(left, right):
    m, n, _ = left.shape
    return call(
        kron_kernel,
        jax.ShapeDtypeStruct((m, 2 * n * n, n * n), BF16),
        [VM, VM], VM, [], 4 * 10**8, 4 * 10**6, "kron",
    )(left, right)


def cut_kernel(at, source, after, out, sem):
    del after
    copy = pltpu.make_async_copy(source.at[:, pl.ds(at, out.shape[1])], out, sem)
    copy.start()
    copy.wait()


def cut(source, at, rows, after):
    shape = (source.shape[0], rows, source.shape[2])
    return call(
        functools.partial(cut_kernel, at),
        jax.ShapeDtypeStruct(shape, source.dtype),
        [ANY, ANY], ANY, [pltpu.SemaphoreType.DMA],
        0, 4 * rows * source.shape[0] * source.shape[2], "cut",
    )(source, after)


def features_kernel(places, ids, *refs):
    pieces, (w_ref, out_ref) = refs[: len(places)], refs[len(places):]
    z, x = ids[0], ids[1]
    modules, rows, width = pieces[0].shape
    slots = [
        lax.rem(z + dz, 2) * 4 + lax.rem(x + dx, 4) for dz, dx in places
    ]
    for m in range(modules):
        g = jnp.concatenate([p[m] for p in pieces], axis=0)
        g = jnp.concatenate([g, g], axis=1)
        f = jnp.dot(g, w_ref[m], preferred_element_type=F32).astype(BF16)
        for k, slot in enumerate(slots):
            out_ref[slot, :, m * width:(m + 1) * width] = f[k * rows:(k + 1) * rows]


def make_features(ids, pieces, w):
    places = tuple(pieces)
    arrays = [pieces[p] for p in places]
    modules, rows, width = arrays[0].shape
    n = len(places)
    return call(
        functools.partial(features_kernel, places),
        jax.ShapeDtypeStruct((n, rows, modules * width), BF16),
        [SM] + [VM] * n + [VM], VM, [],
        4 * n * rows * modules * width * width, 3 * n * rows * modules * width, "features",
    )(ids, *arrays, w)


def product_kernel(shifts, finish, n_out, ids, mine, other, train, *refs):
    outs, (acc,) = refs[:n_out], refs[n_out:]
    core, y = ids[2], ids[3]
    modules, columns, width = train.shape
    rows = mine.shape[1]
    n = 4 * rows

    def run(sources):
        for m in range(modules):
            f = []
            for shift, source in zip(shifts, sources):
                part = lax.rem(y + shift, 4) // 2
                for h in range(4):
                    f.append(source[2 * h + part, :, m * width:(m + 1) * width])
            part = lax.dot_general(
                jnp.concatenate(f, axis=0), train[m], (((1,), (1,)), ((), ())),
                preferred_element_type=F32,
            )
            if m == 0:
                acc[...] = part
            else:
                acc[...] += part

    same = lax.rem(y, 2) == core

    @pl.when(same)
    def _():
        run([other if shift % 2 else mine for shift in shifts])

    @pl.when(jnp.logical_not(same))
    def _():
        run([mine if shift % 2 else other for shift in shifts])

    if finish is not None:
        finish(acc, outs)


def product(shifts, finish, out_shape, ids, mine, other, train, name):
    rows = mine.shape[1]
    depth = mine.shape[2]
    columns = train.shape[1]
    n = len(shifts) * 4 * rows
    if finish is None:
        kernel = functools.partial(product_kernel, shifts, None, 0)
        scratch = []
    else:
        kernel = functools.partial(product_kernel, shifts, finish, len(out_shape))
        scratch = [pltpu.VMEM((n, columns), F32)]
    return call(
        kernel, out_shape, [SM, VM, VM, VM], [VM] * len(out_shape), scratch,
        2 * n * depth * columns, 2 * (n * depth + depth * columns + n * columns), name,
    )(ids, mine, other, train)


def finish_far(acc, outs):
    rows = outs[0].shape[1]
    for h in range(4):
        outs[h // 2][h % 2] = acc[h * rows:(h + 1) * rows].astype(BF16)


def near_kernel(acc, up, down, out_up, out_down):
    rows = up.shape[1]
    for k, (extra, out) in enumerate(((up, out_up), (down, out_down))):
        for h in range(4):
            at = (k * 4 + h) * rows
            part = acc[at:at + rows]
            if h // 2 == k:
                part = part + extra[h % 2].astype(F32)
            out[h] = part.astype(BF16)


def own_kernel(ids, acc, up, down, *outs):
    hi = ids[4]
    rows = up.shape[1]
    for k in range(4):
        h = lax.rem(hi + k, 4)
        at = pl.multiple_of((8 + h) * rows, rows)
        total = acc[pl.ds(at, rows), :] + up[h].astype(F32) + down[h].astype(F32)
        outs[k][...] = total.astype(outs[k].dtype)


def total_kernel(*refs):
    out = refs[-1]
    at = 0
    for k in range(0, len(refs) - 1, 4):
        rows = refs[k].shape[0]
        total = refs[k][...]
        for r in refs[k + 1:k + 4]:
            total = total + r[...].astype(F32)
        out[at:at + rows] = total
        at += rows


def gather_pieces(own):
    send = functools.partial(lax.ppermute, axis_name="ex")
    z = send(own, perm=TO_Z)
    left = send(own, perm=to_x(1))
    right = send(own, perm=to_x(-1))
    far = send(own, perm=to_x(2))
    z_left = send(z, perm=to_x(1))
    z_right = send(z, perm=to_x(-1))
    z_far = send(far, perm=TO_Z)
    return {
        (0, 0): own, (1, 0): z, (0, 3): left, (0, 1): right, (0, 2): far,
        (1, 3): z_left, (1, 1): z_right, (1, 2): z_far,
    }


def body(train_grads, test_grads, left_inv, right_inv):
    ex = lax.axis_index("ex")
    mod = lax.axis_index("mod")
    ids = jnp.stack([ex // 8, (ex // 2) % 4, ex % 2, mod % 4, mod // 4]).astype(jnp.int32)
    columns = train_grads.shape[1]
    w = make_kron(left_inv, right_inv)
    at = 0
    parts = []
    mine = None
    for rows in CHUNKS:
        if mine is None:
            first = test_grads[:, :rows]
        else:
            first = cut(test_grads, at, rows, mine)
        pieces = gather_pieces(first)
        at += rows
        mine = make_features(ids, pieces, w)
        other = lax.ppermute(mine, "ex", TO_CORE)
        half = jax.ShapeDtypeStruct((2, rows, columns), BF16)
        whole = jax.ShapeDtypeStruct((4, rows, columns), BF16)
        one = jax.ShapeDtypeStruct((rows, columns), BF16)
        keep = jax.ShapeDtypeStruct((rows, columns), F32)
        acc = jax.ShapeDtypeStruct((12 * rows, columns), F32)
        up, down = product((2,), finish_far, [half] * 2, ids, mine, other, train_grads, "far")
        up = lax.ppermute(up, "mod", to_y(1))
        down = lax.ppermute(down, "mod", to_y(-1))
        (acc,) = product((1, 3, 0), None, [acc], ids, mine, other, train_grads, "rest")
        up, down = call(
            near_kernel, [whole] * 2, [VM] * 3, [VM] * 2, [],
            2 * rows * columns, 40 * rows * columns, "near",
        )(acc, up, down)
        up = lax.ppermute(up, "mod", to_y(1))
        down = lax.ppermute(down, "mod", to_y(-1))
        own, h1, h2, h3 = call(
            own_kernel, [keep] + [one] * 3, [SM] + [VM] * 3, [VM] * 4, [],
            8 * rows * columns, 40 * rows * columns, "own",
        )(ids, acc, up, down)
        parts += [
            own,
            lax.ppermute(h1, "mod", to_h(1)),
            lax.ppermute(h2, "mod", to_h(2)),
            lax.ppermute(h3, "mod", to_h(3)),
        ]
    rows = test_grads.shape[1]
    return call(
        total_kernel,
        jax.ShapeDtypeStruct((rows, columns), F32),
        [VM] * len(parts), VM, [],
        4 * rows * columns, 16 * rows * columns, "total",
    )(*parts)


def solution(mesh):
    return jax.shard_map(
        body,
        mesh=mesh,
        in_specs=(
            P("mod", "ex", None),
            P("mod", "ex", None),
            P("mod", None, None),
            P("mod", None, None),
        ),
        out_specs=P("mod", "ex"),
        check_vma=False,
    )
```

```python
import functools

import jax
import jax.numpy as jnp
from jax import lax
from jax.experimental import pallas as pl
from jax.experimental.pallas import tpu as pltpu
from jax.sharding import PartitionSpec as P

F32 = jnp.float32
BF16 = jnp.bfloat16
GATHERS = (128,)
CHUNKS = (64, 64)
GROUPS = ((0,), (1,))
ORDER = (
    ("gather", 0), ("forward", 0), ("kron", 0), ("features", 0), ("features", 1),
    ("far", 0), ("far", 1), ("side", 0), ("near", 0), ("side", 1),
    ("near", 1), ("keep", 0), ("keep", 1), ("own", 0), ("own", 1),
    ("total", 0), ("total", 1),
)
VMEM_LIMIT = 20 * 1024 * 1024


def ex_perm(move):
    pairs = []
    for i in range(16):
        z, x, c = i // 8, (i // 2) % 4, i % 2
        z, x, c = move(z, x, c)
        pairs.append((i, ((z % 2) * 4 + x % 4) * 2 + c % 2))
    return pairs


def to_x(d):
    return ex_perm(lambda z, x, c: (z, x + d, c))


TO_Z = ex_perm(lambda z, x, c: (z + 1, x, c))
TO_CORE = ex_perm(lambda z, x, c: (z, x, c + 1))


def mod_perm(move):
    pairs = []
    for i in range(16):
        h, y = move(i // 4, i % 4)
        pairs.append((i, (h % 4) * 4 + y % 4))
    return pairs


def to_y(d):
    return mod_perm(lambda h, y: (h, y + d))


def to_h(d):
    return mod_perm(lambda h, y: (h + d, y))


FAR = [
    (e * 16 + i, e * 16 + j) for e in range(16) for i, j in (to_y(-1) if e % 2 else to_y(1))
]


def call(kernel, out_shape, in_specs, out_specs, scratch, flops, moved, name, aliases=None):
    def run(after, *arrays):
        n = len(in_specs)

        def ordered(*refs):
            kernel(*refs[:n], *refs[n + len(after):])

        return pl.pallas_call(
            ordered,
            out_shape=out_shape,
            in_specs=in_specs + [VM] * len(after),
            out_specs=out_specs,
            scratch_shapes=scratch,
            input_output_aliases=aliases or {},
            compiler_params=pltpu.CompilerParams(vmem_limit_bytes=VMEM_LIMIT),
            cost_estimate=pl.CostEstimate(flops=flops, bytes_accessed=moved, transcendentals=0),
            name=name,
        )(*arrays, *after)

    return run


VM = pl.BlockSpec(memory_space=pltpu.VMEM)
SM = pl.BlockSpec(memory_space=pltpu.SMEM)
ANY = pl.BlockSpec(memory_space=pl.ANY)


def kron_kernel(left_ref, right_ref, w_ref):
    width = left_ref.shape[1]
    full = width * width
    wide = lax.broadcasted_iota(jnp.int32, (width, full), 1)
    narrow = lax.broadcasted_iota(jnp.int32, (width, full), 0)
    outer = jnp.where(wide // width == narrow, 1.0, 0.0).astype(F32)
    inner = jnp.where(wide % width == narrow, 1.0, 0.0).astype(F32)
    dot = functools.partial(
        lax.dot_general, precision=lax.Precision.HIGHEST, preferred_element_type=F32
    )
    for m in range(left_ref.shape[0]):
        l1 = dot(left_ref[m], outer, (((0,), (0,)), ((), ())))
        lx = dot(outer, l1, (((0,), (0,)), ((), ())))
        r1 = dot(right_ref[m], inner, (((1,), (0,)), ((), ())))
        rx = dot(inner, r1, (((0,), (0,)), ((), ())))
        w = lx * rx
        high = w.astype(BF16)
        w_ref[m, :full] = high
        w_ref[m, full:] = (w - high.astype(F32)).astype(BF16)


def make_kron(left, right, after):
    m, n, _ = left.shape
    return call(
        kron_kernel,
        jax.ShapeDtypeStruct((m, 2 * n * n, n * n), BF16),
        [VM, VM], VM, [], 4 * 10**8, 4 * 10**6, "kron",
    )(after, left, right)


def gate_kernel(*refs):
    del refs


def gate(arrays, after):
    n = len(arrays)
    return call(
        gate_kernel,
        [jax.ShapeDtypeStruct(a.shape, a.dtype) for a in arrays],
        [VM] * n, [VM] * n, [], 0, 0, "gate", {i: i for i in range(n)},
    )(after, *arrays)


def features_kernel(places, at, ids, *refs):
    pieces, (w_ref, out_ref) = refs[: len(places)], refs[len(places):]
    z, x = ids[0], ids[1]
    modules, _, width = pieces[0].shape
    rows = out_ref.shape[1]
    slots = [
        lax.rem(z + dz, 2) * 4 + lax.rem(x + dx, 4) for dz, dx in places
    ]
    for m in range(modules):
        g = jnp.concatenate([p[m, at:at + rows] for p in pieces], axis=0)
        g = jnp.concatenate([g, g], axis=1)
        f = jnp.dot(g, w_ref[m], preferred_element_type=F32).astype(BF16)
        for k, slot in enumerate(slots):
            out_ref[slot, :, m * width:(m + 1) * width] = f[k * rows:(k + 1) * rows]


def make_features(ids, pieces, at, rows, w, after):
    places = tuple(pieces)
    arrays = [pieces[p] for p in places]
    modules, _, width = arrays[0].shape
    n = len(places)
    return call(
        functools.partial(features_kernel, places, at),
        jax.ShapeDtypeStruct((n, rows, modules * width), BF16),
        [SM] + [VM] * n + [VM], VM, [],
        4 * n * rows * modules * width * width, 3 * n * rows * modules * width, "features",
    )(after, ids, *arrays, w)


def product_kernel(shifts, finish, n_out, ids, mine, other, train, *refs):
    outs, (acc,) = refs[:n_out], refs[n_out:]
    core, y = ids[2], ids[3]
    modules, columns, width = train.shape

    def run(sources):
        for m in range(modules):
            f = []
            for shift, source in zip(shifts, sources):
                half = lax.rem(y + shift, 4) // 2
                for h in range(4):
                    f.append(source[2 * h + half, :, m * width:(m + 1) * width])
            part = lax.dot_general(
                jnp.concatenate(f, axis=0), train[m], (((1,), (1,)), ((), ())),
                preferred_element_type=F32,
            )
            if m == 0:
                acc[...] = part
            else:
                acc[...] += part

    same = lax.rem(y, 2) == core

    @pl.when(same)
    def _():
        run([other if shift % 2 else mine for shift in shifts])

    @pl.when(jnp.logical_not(same))
    def _():
        run([mine if shift % 2 else other for shift in shifts])

    if finish is not None:
        finish(acc, outs)


def product(shifts, finish, out_shape, ids, mine, other, train, name, after):
    rows = mine.shape[1]
    depth = mine.shape[2]
    columns = train.shape[1]
    n = len(shifts) * 4 * rows
    if finish is None:
        kernel = functools.partial(product_kernel, shifts, None, 0)
        scratch = []
    else:
        kernel = functools.partial(product_kernel, shifts, finish, len(out_shape))
        scratch = [pltpu.VMEM((n, columns), F32)]
    return call(
        kernel, out_shape, [SM, VM, VM, VM], [VM] * len(out_shape), scratch,
        2 * n * depth * columns, 2 * (n * depth + depth * columns + n * columns), name,
    )(after, ids, mine, other, train)


def finish_far(acc, outs):
    (out,) = outs
    rows = out.shape[1]
    for h in range(4):
        out[h] = acc[h * rows:(h + 1) * rows].astype(BF16)


def near_kernel(ids, acc, got, up, down):
    core = ids[2]
    rows = got.shape[1]
    for k, out in enumerate((up, down)):
        for h in range(4):
            at = (4 * k + h) * rows
            extra = jnp.where(core == k, got[h].astype(F32), 0.0)
            out[h] = (acc[at:at + rows] + extra).astype(BF16)


def own_kernel(n, ids, *refs):
    ins, outs = refs[:3 * n], refs[3 * n:]
    hi = ids[4]
    to = 0
    for i in range(n):
        acc, up, down = ins[3 * i:3 * i + 3]
        rows = up.shape[1]
        for k in range(4):
            h = lax.rem(hi + k, 4)
            at = pl.multiple_of(h * rows, rows)
            total = acc[pl.ds(at, rows), :] + up[h].astype(F32) + down[h].astype(F32)
            outs[k][to:to + rows] = total.astype(outs[k].dtype)
        to += rows


def total_kernel(at, own, h1, h2, h3, *refs):
    *_, out, total, sem = refs
    total[...] = own[...] + h1[...].astype(F32) + h2[...].astype(F32) + h3[...].astype(F32)
    copy = pltpu.make_async_copy(total, out.at[pl.ds(at, own.shape[0])], sem)
    copy.start()
    copy.wait()


class Steps:
    def __init__(self, ids, train, test, factors):
        self.ids, self.train, self.test, self.factors = ids, train, test, factors
        self.columns = train.shape[1]
        self.pieces, self.mine, self.other = {}, {}, {}
        self.acc, self.got, self.kept = {}, {}, {}
        self.up, self.down, self.parts = {}, {}, {}
        self.out = None

    def gather(self, g, after):
        at = sum(GATHERS[:g])
        own = self.test[:, at:at + GATHERS[g]]
        if after:
            (own,) = gate([own], after)
        send = functools.partial(lax.ppermute, axis_name="ex")
        self.pieces[g] = {
            (0, 0): own,
            (1, 0): send(own, perm=TO_Z),
            (0, 2): send(own, perm=to_x(2)),
            (0, 3): send(own, perm=to_x(1)),
            (0, 1): send(own, perm=to_x(-1)),
        }
        return None

    def forward(self, g, after):
        pieces = self.pieces[g]
        z, far = pieces[1, 0], pieces[0, 2]
        if after:
            z, far = gate([z, far], after)
        send = functools.partial(lax.ppermute, axis_name="ex")
        pieces[1, 0], pieces[0, 2] = z, far
        pieces[1, 3] = send(z, perm=to_x(1))
        pieces[1, 1] = send(z, perm=to_x(-1))
        pieces[1, 2] = send(far, perm=TO_Z)
        return z

    def kron(self, _, after):
        self.w = make_kron(*self.factors, after)
        return self.w

    def features(self, c, after):
        at, g = sum(CHUNKS[:c]), 0
        while at >= GATHERS[g]:
            at, g = at - GATHERS[g], g + 1
        self.mine[c] = make_features(self.ids, self.pieces[g], at, CHUNKS[c], self.w, after)
        self.other[c] = lax.ppermute(self.mine[c], "ex", TO_CORE)
        return self.mine[c]

    def far(self, c, after):
        out = jax.ShapeDtypeStruct((4, CHUNKS[c], self.columns), BF16)
        (out,) = product(
            (2,), finish_far, [out], self.ids, self.mine[c], self.other[c], self.train, "far", after
        )
        self.got[c] = lax.ppermute(out, ("ex", "mod"), FAR)
        return out

    def side(self, c, after):
        acc = jax.ShapeDtypeStruct((8 * CHUNKS[c], self.columns), F32)
        (self.acc[c],) = product(
            (1, 3), None, [acc], self.ids, self.mine[c], self.other[c], self.train, "side", after
        )
        return self.acc[c]

    def keep(self, c, after):
        acc = jax.ShapeDtypeStruct((4 * CHUNKS[c], self.columns), F32)
        (self.kept[c],) = product(
            (0,), None, [acc], self.ids, self.mine[c], self.other[c], self.train, "keep", after
        )
        return self.kept[c]

    def near(self, c, after):
        rows, columns = CHUNKS[c], self.columns
        up, down = call(
            near_kernel, [jax.ShapeDtypeStruct((4, rows, columns), BF16)] * 2,
            [SM] + [VM] * 2, [VM] * 2, [],
            rows * columns, 20 * rows * columns, "near",
        )(after, self.ids, self.acc[c], self.got[c])
        self.up[c] = lax.ppermute(up, "mod", to_y(1))
        self.down[c] = lax.ppermute(down, "mod", to_y(-1))
        return up

    def own(self, group, after):
        members, columns = GROUPS[group], self.columns
        rows = sum(CHUNKS[c] for c in members)
        ins = [a[c] for c in members for a in (self.kept, self.up, self.down)]
        one = jax.ShapeDtypeStruct((rows, columns), BF16)
        stays = jax.ShapeDtypeStruct((rows, columns), F32)
        own, h1, h2, h3 = call(
            functools.partial(own_kernel, len(members)), [stays] + [one] * 3,
            [SM] + [VM] * len(ins), [VM] * 4, [],
            8 * rows * columns, 40 * rows * columns, "own",
        )(after, self.ids, *ins)
        send = functools.partial(lax.ppermute, axis_name="mod")
        h2 = send(h2, perm=to_h(2))
        self.parts[group] = [own, send(h1, perm=to_h(1)), h2, send(h3, perm=to_h(3))]
        return own

    def total(self, group, after):
        at = sum(CHUNKS[:GROUPS[group][0]])
        parts = self.parts[group]
        rows, columns = parts[0].shape
        before = [] if self.out is None else [self.out]
        self.out = call(
            functools.partial(total_kernel, at),
            jax.ShapeDtypeStruct((self.test.shape[1], columns), F32),
            [VM] * 4 + [ANY] * len(before), ANY,
            [pltpu.VMEM((rows, columns), F32), pltpu.SemaphoreType.DMA],
            4 * rows * columns, 16 * rows * columns, "total", {4: 0} if before else {},
        )(after, *parts, *before)
        return parts[0]


def body(train_grads, test_grads, left_inv, right_inv):
    ex = lax.axis_index("ex")
    mod = lax.axis_index("mod")
    ids = jnp.stack([ex // 8, (ex // 2) % 4, ex % 2, mod % 4, mod // 4]).astype(jnp.int32)
    steps = Steps(ids, train_grads, test_grads, (left_inv, right_inv))
    after = []
    for name, which in ORDER:
        done = getattr(steps, name)(which, after)
        after = after if done is None else [done]
    return steps.out


def solution(mesh):
    return jax.shard_map(
        body,
        mesh=mesh,
        in_specs=(
            P("mod", "ex", None),
            P("mod", "ex", None),
            P("mod", None, None),
            P("mod", None, None),
        ),
        out_specs=P("mod", "ex"),
        check_vma=False,
    )
```

```python
import functools

import jax
import jax.numpy as jnp
from jax import lax
from jax.experimental import pallas as pl
from jax.experimental.pallas import tpu as pltpu
from jax.sharding import PartitionSpec as P

F32 = jnp.float32
BF16 = jnp.bfloat16
GATHERS = (128,)
CHUNKS = (64, 64)
GROUPS = ((0,), (1,))
ORDER = (
    ("gather", 0), ("forward", 0), ("kron", 0), ("features", 0), ("features", 1),
    ("far", 0), ("far", 1), ("side", 0), ("near", 0), ("side", 1),
    ("near", 1), ("keep", 0), ("keep", 1), ("own", 0), ("own", 1),
    ("total", 0), ("total", 1),
)
VMEM_LIMIT = 20 * 1024 * 1024


def ex_perm(move):
    pairs = []
    for i in range(16):
        z, x, c = i // 8, (i // 2) % 4, i % 2
        z, x, c = move(z, x, c)
        pairs.append((i, ((z % 2) * 4 + x % 4) * 2 + c % 2))
    return pairs


def to_x(d):
    return ex_perm(lambda z, x, c: (z, x + d, c))


TO_Z = ex_perm(lambda z, x, c: (z + 1, x, c))
TO_CORE = ex_perm(lambda z, x, c: (z, x, c + 1))


def mod_perm(move):
    pairs = []
    for i in range(16):
        h, y = move(i // 4, i % 4)
        pairs.append((i, (h % 4) * 4 + y % 4))
    return pairs


def to_y(d):
    return mod_perm(lambda h, y: (h, y + d))


def to_h(d):
    return mod_perm(lambda h, y: (h + d, y))


FAR = [
    (e * 16 + i, e * 16 + j) for e in range(16) for i, j in (to_y(-1) if e % 2 else to_y(1))
]


def call(kernel, out_shape, in_specs, out_specs, scratch, flops, moved, name, aliases=None):
    def run(after, *arrays):
        n = len(in_specs)

        def ordered(*refs):
            kernel(*refs[:n], *refs[n + len(after):])

        return pl.pallas_call(
            ordered,
            out_shape=out_shape,
            in_specs=in_specs + [VM] * len(after),
            out_specs=out_specs,
            scratch_shapes=scratch,
            input_output_aliases=aliases or {},
            compiler_params=pltpu.CompilerParams(vmem_limit_bytes=VMEM_LIMIT),
            cost_estimate=pl.CostEstimate(flops=flops, bytes_accessed=moved, transcendentals=0),
            name=name,
        )(*arrays, *after)

    return run


VM = pl.BlockSpec(memory_space=pltpu.VMEM)
SM = pl.BlockSpec(memory_space=pltpu.SMEM)
ANY = pl.BlockSpec(memory_space=pl.ANY)


def kron_kernel(left_ref, right_ref, w_ref):
    width = left_ref.shape[1]
    full = width * width
    wide = lax.broadcasted_iota(jnp.int32, (width, full), 1)
    narrow = lax.broadcasted_iota(jnp.int32, (width, full), 0)
    outer = jnp.where(wide // width == narrow, 1.0, 0.0).astype(F32)
    inner = jnp.where(wide % width == narrow, 1.0, 0.0).astype(F32)
    dot = functools.partial(
        lax.dot_general, precision=lax.Precision.HIGHEST, preferred_element_type=F32
    )
    for m in range(left_ref.shape[0]):
        l1 = dot(left_ref[m], outer, (((0,), (0,)), ((), ())))
        lx = dot(outer, l1, (((0,), (0,)), ((), ())))
        r1 = dot(right_ref[m], inner, (((1,), (0,)), ((), ())))
        rx = dot(inner, r1, (((0,), (0,)), ((), ())))
        w = lx * rx
        high = w.astype(BF16)
        w_ref[m, :full] = high
        w_ref[m, full:] = (w - high.astype(F32)).astype(BF16)


def make_kron(left, right, after):
    m, n, _ = left.shape
    return call(
        kron_kernel,
        jax.ShapeDtypeStruct((m, 2 * n * n, n * n), BF16),
        [VM, VM], VM, [], 4 * 10**8, 4 * 10**6, "kron",
    )(after, left, right)


def gate_kernel(*refs):
    del refs


def gate(arrays, after):
    n = len(arrays)
    return call(
        gate_kernel,
        [jax.ShapeDtypeStruct(a.shape, a.dtype) for a in arrays],
        [VM] * n, [VM] * n, [], 0, 0, "gate", {i: i for i in range(n)},
    )(after, *arrays)


def features_kernel(places, at, ids, *refs):
    pieces, (w_ref, out_ref) = refs[: len(places)], refs[len(places):]
    z, x = ids[0], ids[1]
    modules, _, width = pieces[0].shape
    rows = out_ref.shape[1]
    slots = [
        lax.rem(z + dz, 2) * 4 + lax.rem(x + dx, 4) for dz, dx in places
    ]
    for m in range(modules):
        g = jnp.concatenate([p[m, at:at + rows] for p in pieces], axis=0)
        g = jnp.concatenate([g, g], axis=1)
        f = jnp.dot(g, w_ref[m], preferred_element_type=F32).astype(BF16)
        for k, slot in enumerate(slots):
            out_ref[slot, :, m * width:(m + 1) * width] = f[k * rows:(k + 1) * rows]


def make_features(ids, pieces, at, rows, w, after):
    places = tuple(pieces)
    arrays = [pieces[p] for p in places]
    modules, _, width = arrays[0].shape
    n = len(places)
    return call(
        functools.partial(features_kernel, places, at),
        jax.ShapeDtypeStruct((n, rows, modules * width), BF16),
        [SM] + [VM] * n + [VM], VM, [],
        4 * n * rows * modules * width * width, 3 * n * rows * modules * width, "features",
    )(after, ids, *arrays, w)


def product_kernel(shifts, finish, n_out, ids, mine, other, train, *refs):
    outs, (acc,) = refs[:n_out], refs[n_out:]
    core, y = ids[2], ids[3]
    modules, columns, width = train.shape

    def run(sources):
        for m in range(modules):
            f = []
            for shift, source in zip(shifts, sources):
                half = lax.rem(y + shift, 4) // 2
                for h in range(4):
                    f.append(source[2 * h + half, :, m * width:(m + 1) * width])
            part = lax.dot_general(
                jnp.concatenate(f, axis=0), train[m], (((1,), (1,)), ((), ())),
                preferred_element_type=F32,
            )
            if m == 0:
                acc[...] = part
            else:
                acc[...] += part

    same = lax.rem(y, 2) == core

    @pl.when(same)
    def _():
        run([other if shift % 2 else mine for shift in shifts])

    @pl.when(jnp.logical_not(same))
    def _():
        run([mine if shift % 2 else other for shift in shifts])

    if finish is not None:
        finish(acc, outs)


def product(shifts, finish, out_shape, ids, mine, other, train, name, after):
    rows = mine.shape[1]
    depth = mine.shape[2]
    columns = train.shape[1]
    n = len(shifts) * 4 * rows
    if finish is None:
        kernel = functools.partial(product_kernel, shifts, None, 0)
        scratch = []
    else:
        kernel = functools.partial(product_kernel, shifts, finish, len(out_shape))
        scratch = [pltpu.VMEM((n, columns), F32)]
    return call(
        kernel, out_shape, [SM, VM, VM, VM], [VM] * len(out_shape), scratch,
        2 * n * depth * columns, 2 * (n * depth + depth * columns + n * columns), name,
    )(after, ids, mine, other, train)


def finish_far(acc, outs):
    (out,) = outs
    rows = out.shape[1]
    for h in range(4):
        out[h] = acc[h * rows:(h + 1) * rows].astype(BF16)


def near_kernel(ids, acc, got, up, down):
    core = ids[2]
    rows = got.shape[1]
    for k, out in enumerate((up, down)):
        for h in range(4):
            at = (4 * k + h) * rows
            extra = jnp.where(core == k, got[h].astype(F32), 0.0)
            out[h] = (acc[at:at + rows] + extra).astype(BF16)


def own_kernel(n, ids, *refs):
    ins, outs = refs[:3 * n], refs[3 * n:]
    hi = ids[4]
    to = 0
    for i in range(n):
        acc, up, down = ins[3 * i:3 * i + 3]
        rows = up.shape[1]
        for k in range(4):
            h = lax.rem(hi + k, 4)
            at = pl.multiple_of(h * rows, rows)
            total = acc[pl.ds(at, rows), :] + up[h].astype(F32) + down[h].astype(F32)
            outs[k][to:to + rows] = total.astype(outs[k].dtype)
        to += rows


def total_kernel(at, own, h1, h2, h3, *refs):
    *_, out, total, sem = refs
    total[...] = own[...] + h1[...].astype(F32) + h2[...].astype(F32) + h3[...].astype(F32)
    copy = pltpu.make_async_copy(total, out.at[pl.ds(at, own.shape[0])], sem)
    copy.start()
    copy.wait()


class Steps:
    def __init__(self, ids, train, test, factors):
        self.ids, self.train, self.test, self.factors = ids, train, test, factors
        self.columns = train.shape[1]
        self.pieces, self.mine, self.other = {}, {}, {}
        self.acc, self.got, self.kept = {}, {}, {}
        self.up, self.down, self.parts = {}, {}, {}
        self.out = None

    def gather(self, g, after):
        at = sum(GATHERS[:g])
        own = self.test[:, at:at + GATHERS[g]]
        if after:
            (own,) = gate([own], after)
        send = functools.partial(lax.ppermute, axis_name="ex")
        self.pieces[g] = {
            (0, 0): own,
            (1, 0): send(own, perm=TO_Z),
            (0, 2): send(own, perm=to_x(2)),
            (0, 3): send(own, perm=to_x(1)),
            (0, 1): send(own, perm=to_x(-1)),
        }
        return None

    def forward(self, g, after):
        pieces = self.pieces[g]
        z, far = pieces[1, 0], pieces[0, 2]
        if after:
            z, far = gate([z, far], after)
        send = functools.partial(lax.ppermute, axis_name="ex")
        pieces[1, 0], pieces[0, 2] = z, far
        pieces[1, 3] = send(z, perm=to_x(1))
        pieces[1, 1] = send(z, perm=to_x(-1))
        pieces[1, 2] = send(far, perm=TO_Z)
        return z

    def kron(self, _, after):
        self.w = make_kron(*self.factors, after)
        return self.w

    def features(self, c, after):
        at, g = sum(CHUNKS[:c]), 0
        while at >= GATHERS[g]:
            at, g = at - GATHERS[g], g + 1
        self.mine[c] = make_features(self.ids, self.pieces[g], at, CHUNKS[c], self.w, after)
        self.other[c] = lax.ppermute(self.mine[c], "ex", TO_CORE)
        return self.mine[c]

    def far(self, c, after):
        out = jax.ShapeDtypeStruct((4, CHUNKS[c], self.columns), BF16)
        (out,) = product(
            (2,), finish_far, [out], self.ids, self.mine[c], self.other[c], self.train, "far", after
        )
        self.got[c] = lax.ppermute(out, ("ex", "mod"), FAR)
        return out

    def side(self, c, after):
        acc = jax.ShapeDtypeStruct((8 * CHUNKS[c], self.columns), F32)
        (self.acc[c],) = product(
            (1, 3), None, [acc], self.ids, self.mine[c], self.other[c], self.train, "side", after
        )
        return self.acc[c]

    def keep(self, c, after):
        acc = jax.ShapeDtypeStruct((4 * CHUNKS[c], self.columns), F32)
        (self.kept[c],) = product(
            (0,), None, [acc], self.ids, self.mine[c], self.other[c], self.train, "keep", after
        )
        return self.kept[c]

    def near(self, c, after):
        rows, columns = CHUNKS[c], self.columns
        up, down = call(
            near_kernel, [jax.ShapeDtypeStruct((4, rows, columns), BF16)] * 2,
            [SM] + [VM] * 2, [VM] * 2, [],
            rows * columns, 20 * rows * columns, "near",
        )(after, self.ids, self.acc[c], self.got[c])
        self.up[c] = lax.ppermute(up, "mod", to_y(1))
        self.down[c] = lax.ppermute(down, "mod", to_y(-1))
        return up

    def own(self, group, after):
        members, columns = GROUPS[group], self.columns
        rows = sum(CHUNKS[c] for c in members)
        ins = [a[c] for c in members for a in (self.kept, self.up, self.down)]
        one = jax.ShapeDtypeStruct((rows, columns), BF16)
        stays = jax.ShapeDtypeStruct((rows, columns), F32)
        own, h1, h2, h3 = call(
            functools.partial(own_kernel, len(members)), [stays] + [one] * 3,
            [SM] + [VM] * len(ins), [VM] * 4, [],
            8 * rows * columns, 40 * rows * columns, "own",
        )(after, self.ids, *ins)
        send = functools.partial(lax.ppermute, axis_name="mod")
        h2 = send(h2, perm=to_h(2))
        self.parts[group] = [own, h2, send(h1, perm=to_h(1)), send(h3, perm=to_h(3))]
        return own

    def total(self, group, after):
        at = sum(CHUNKS[:GROUPS[group][0]])
        parts = self.parts[group]
        rows, columns = parts[0].shape
        before = [] if self.out is None else [self.out]
        self.out = call(
            functools.partial(total_kernel, at),
            jax.ShapeDtypeStruct((self.test.shape[1], columns), F32),
            [VM] * 4 + [ANY] * len(before), ANY,
            [pltpu.VMEM((rows, columns), F32), pltpu.SemaphoreType.DMA],
            4 * rows * columns, 16 * rows * columns, "total", {4: 0} if before else {},
        )(after, *parts, *before)
        return parts[0]


def body(train_grads, test_grads, left_inv, right_inv):
    ex = lax.axis_index("ex")
    mod = lax.axis_index("mod")
    ids = jnp.stack([ex // 8, (ex // 2) % 4, ex % 2, mod % 4, mod // 4]).astype(jnp.int32)
    steps = Steps(ids, train_grads, test_grads, (left_inv, right_inv))
    after = []
    for name, which in ORDER:
        done = getattr(steps, name)(which, after)
        after = after if done is None else [done]
    return steps.out


def solution(mesh):
    return jax.shard_map(
        body,
        mesh=mesh,
        in_specs=(
            P("mod", "ex", None),
            P("mod", "ex", None),
            P("mod", None, None),
            P("mod", None, None),
        ),
        out_specs=P("mod", "ex"),
        check_vma=False,
    )
```

```python
import functools

import jax
import jax.numpy as jnp
from jax import lax
from jax.experimental import pallas as pl
from jax.experimental.pallas import tpu as pltpu
from jax.sharding import PartitionSpec as P

F32 = jnp.float32
BF16 = jnp.bfloat16
GATHERS = (128,)
CHUNKS = (64, 64)
GROUPS = ((0,), (1,))
ORDER = (
    ("gather", 0), ("forward", 0), ("kron", 0), ("features", 0), ("features", 1),
    ("far", 0), ("far", 1), ("side", 0), ("near", 0), ("side", 1),
    ("near", 1), ("keep", 0), ("keep", 1), ("own", 0), ("own", 1),
    ("total", 0), ("total", 1),
)
VMEM_LIMIT = 20 * 1024 * 1024


def ex_perm(move):
    pairs = []
    for i in range(16):
        z, x, c = i // 8, (i // 2) % 4, i % 2
        z, x, c = move(z, x, c)
        pairs.append((i, ((z % 2) * 4 + x % 4) * 2 + c % 2))
    return pairs


def to_x(d):
    return ex_perm(lambda z, x, c: (z, x + d, c))


TO_Z = ex_perm(lambda z, x, c: (z + 1, x, c))
TO_CORE = ex_perm(lambda z, x, c: (z, x, c + 1))


def mod_perm(move):
    pairs = []
    for i in range(16):
        h, y = move(i // 4, i % 4)
        pairs.append((i, (h % 4) * 4 + y % 4))
    return pairs


def to_y(d):
    return mod_perm(lambda h, y: (h, y + d))


def to_h(d):
    return mod_perm(lambda h, y: (h + d, y))


FAR = [
    (e * 16 + i, e * 16 + j) for e in range(16) for i, j in (to_y(-1) if e % 2 else to_y(1))
]


def call(kernel, out_shape, in_specs, out_specs, scratch, flops, moved, name, aliases=None):
    def run(after, *arrays):
        n = len(in_specs)

        def ordered(*refs):
            kernel(*refs[:n], *refs[n + len(after):])

        return pl.pallas_call(
            ordered,
            out_shape=out_shape,
            in_specs=in_specs + [VM] * len(after),
            out_specs=out_specs,
            scratch_shapes=scratch,
            input_output_aliases=aliases or {},
            compiler_params=pltpu.CompilerParams(vmem_limit_bytes=VMEM_LIMIT),
            cost_estimate=pl.CostEstimate(flops=flops, bytes_accessed=moved, transcendentals=0),
            name=name,
        )(*arrays, *after)

    return run


VM = pl.BlockSpec(memory_space=pltpu.VMEM)
SM = pl.BlockSpec(memory_space=pltpu.SMEM)
ANY = pl.BlockSpec(memory_space=pl.ANY)


def kron_kernel(left_ref, right_ref, w_ref):
    width = left_ref.shape[1]
    full = width * width
    wide = lax.broadcasted_iota(jnp.int32, (width, full), 1)
    narrow = lax.broadcasted_iota(jnp.int32, (width, full), 0)
    outer = jnp.where(wide // width == narrow, 1.0, 0.0).astype(F32)
    inner = jnp.where(wide % width == narrow, 1.0, 0.0).astype(F32)
    dot = functools.partial(
        lax.dot_general, precision=lax.Precision.HIGHEST, preferred_element_type=F32
    )
    for m in range(left_ref.shape[0]):
        l1 = dot(left_ref[m], outer, (((0,), (0,)), ((), ())))
        lx = dot(outer, l1, (((0,), (0,)), ((), ())))
        r1 = dot(right_ref[m], inner, (((1,), (0,)), ((), ())))
        rx = dot(inner, r1, (((0,), (0,)), ((), ())))
        w = lx * rx
        high = w.astype(BF16)
        w_ref[m, :full] = high
        w_ref[m, full:] = (w - high.astype(F32)).astype(BF16)


def make_kron(left, right, after):
    m, n, _ = left.shape
    return call(
        kron_kernel,
        jax.ShapeDtypeStruct((m, 2 * n * n, n * n), BF16),
        [VM, VM], VM, [], 4 * 10**8, 4 * 10**6, "kron",
    )(after, left, right)


def gate_kernel(*refs):
    del refs


def gate(arrays, after):
    n = len(arrays)
    return call(
        gate_kernel,
        [jax.ShapeDtypeStruct(a.shape, a.dtype) for a in arrays],
        [VM] * n, [VM] * n, [], 0, 0, "gate", {i: i for i in range(n)},
    )(after, *arrays)


def features_kernel(places, at, ids, *refs):
    pieces, (w_ref, out_ref) = refs[: len(places)], refs[len(places):]
    z, x = ids[0], ids[1]
    modules, _, width = pieces[0].shape
    rows = out_ref.shape[1]
    slots = [
        lax.rem(z + dz, 2) * 4 + lax.rem(x + dx, 4) for dz, dx in places
    ]
    for m in range(modules):
        g = jnp.concatenate([p[m, at:at + rows] for p in pieces], axis=0)
        g = jnp.concatenate([g, g], axis=1)
        f = jnp.dot(g, w_ref[m], preferred_element_type=F32).astype(BF16)
        for k, slot in enumerate(slots):
            out_ref[slot, :, m * width:(m + 1) * width] = f[k * rows:(k + 1) * rows]


def make_features(ids, pieces, at, rows, w, after):
    places = tuple(pieces)
    arrays = [pieces[p] for p in places]
    modules, _, width = arrays[0].shape
    n = len(places)
    return call(
        functools.partial(features_kernel, places, at),
        jax.ShapeDtypeStruct((n, rows, modules * width), BF16),
        [SM] + [VM] * n + [VM], VM, [],
        4 * n * rows * modules * width * width, 3 * n * rows * modules * width, "features",
    )(after, ids, *arrays, w)


def product_kernel(shifts, finish, n_out, ids, mine, other, train, *refs):
    outs, (acc,) = refs[:n_out], refs[n_out:]
    core, y = ids[2], ids[3]
    modules, columns, width = train.shape

    def run(sources):
        for m in range(modules):
            f = []
            for shift, source in zip(shifts, sources):
                half = lax.rem(y + shift, 4) // 2
                for h in range(4):
                    f.append(source[2 * h + half, :, m * width:(m + 1) * width])
            part = lax.dot_general(
                jnp.concatenate(f, axis=0), train[m], (((1,), (1,)), ((), ())),
                preferred_element_type=F32,
            )
            if m == 0:
                acc[...] = part
            else:
                acc[...] += part

    same = lax.rem(y, 2) == core

    @pl.when(same)
    def _():
        run([other if shift % 2 else mine for shift in shifts])

    @pl.when(jnp.logical_not(same))
    def _():
        run([mine if shift % 2 else other for shift in shifts])

    if finish is not None:
        finish(acc, outs)


def product(shifts, finish, out_shape, ids, mine, other, train, name, after):
    rows = mine.shape[1]
    depth = mine.shape[2]
    columns = train.shape[1]
    n = len(shifts) * 4 * rows
    if finish is None:
        kernel = functools.partial(product_kernel, shifts, None, 0)
        scratch = []
    else:
        kernel = functools.partial(product_kernel, shifts, finish, len(out_shape))
        scratch = [pltpu.VMEM((n, columns), F32)]
    return call(
        kernel, out_shape, [SM, VM, VM, VM], [VM] * len(out_shape), scratch,
        2 * n * depth * columns, 2 * (n * depth + depth * columns + n * columns), name,
    )(after, ids, mine, other, train)


def finish_far(acc, outs):
    (out,) = outs
    rows = out.shape[1]
    for h in range(4):
        out[h] = acc[h * rows:(h + 1) * rows].astype(BF16)


def near_kernel(ids, acc, got, up, down):
    core = ids[2]
    rows = got.shape[1]
    for k, out in enumerate((up, down)):
        for h in range(4):
            at = (4 * k + h) * rows
            extra = jnp.where(core == k, got[h].astype(F32), 0.0)
            out[h] = (acc[at:at + rows] + extra).astype(BF16)


def own_kernel(n, ids, *refs):
    ins, outs = refs[:3 * n], refs[3 * n:]
    hi = ids[4]
    to = 0
    for i in range(n):
        acc, up, down = ins[3 * i:3 * i + 3]
        rows = up.shape[1]
        for k in range(4):
            h = lax.rem(hi + k, 4)
            at = pl.multiple_of(h * rows, rows)
            total = acc[pl.ds(at, rows), :] + up[h].astype(F32) + down[h].astype(F32)
            outs[k][to:to + rows] = total.astype(outs[k].dtype)
        to += rows


def total_kernel(at, own, h1, h2, h3, *refs):
    *_, out, total, sem = refs
    total[...] = own[...] + h1[...].astype(F32) + h2[...].astype(F32) + h3[...].astype(F32)
    copy = pltpu.make_async_copy(total, out.at[pl.ds(at, own.shape[0])], sem)
    copy.start()
    copy.wait()


class Steps:
    def __init__(self, ids, train, test, factors):
        self.ids, self.train, self.test, self.factors = ids, train, test, factors
        self.columns = train.shape[1]
        self.pieces, self.mine, self.other = {}, {}, {}
        self.acc, self.got, self.kept = {}, {}, {}
        self.up, self.down, self.parts = {}, {}, {}
        self.out = None

    def gather(self, g, after):
        at = sum(GATHERS[:g])
        own = self.test[:, at:at + GATHERS[g]]
        if after:
            (own,) = gate([own], after)
        send = functools.partial(lax.ppermute, axis_name="ex")
        self.pieces[g] = {
            (0, 0): own,
            (1, 0): send(own, perm=TO_Z),
            (0, 2): send(own, perm=to_x(2)),
            (0, 3): send(own, perm=to_x(1)),
            (0, 1): send(own, perm=to_x(-1)),
        }
        return None

    def forward(self, g, after):
        pieces = self.pieces[g]
        z, far = pieces[1, 0], pieces[0, 2]
        if after:
            z, far = gate([z, far], after)
        send = functools.partial(lax.ppermute, axis_name="ex")
        pieces[1, 0], pieces[0, 2] = z, far
        pieces[1, 2] = send(far, perm=TO_Z)
        pieces[1, 3] = send(z, perm=to_x(1))
        pieces[1, 1] = send(z, perm=to_x(-1))
        return z

    def kron(self, _, after):
        self.w = make_kron(*self.factors, after)
        return self.w

    def features(self, c, after):
        at, g = sum(CHUNKS[:c]), 0
        while at >= GATHERS[g]:
            at, g = at - GATHERS[g], g + 1
        self.mine[c] = make_features(self.ids, self.pieces[g], at, CHUNKS[c], self.w, after)
        self.other[c] = lax.ppermute(self.mine[c], "ex", TO_CORE)
        return self.mine[c]

    def far(self, c, after):
        out = jax.ShapeDtypeStruct((4, CHUNKS[c], self.columns), BF16)
        (out,) = product(
            (2,), finish_far, [out], self.ids, self.mine[c], self.other[c], self.train, "far", after
        )
        self.got[c] = lax.ppermute(out, ("ex", "mod"), FAR)
        return out

    def side(self, c, after):
        acc = jax.ShapeDtypeStruct((8 * CHUNKS[c], self.columns), F32)
        (self.acc[c],) = product(
            (1, 3), None, [acc], self.ids, self.mine[c], self.other[c], self.train, "side", after
        )
        return self.acc[c]

    def keep(self, c, after):
        acc = jax.ShapeDtypeStruct((4 * CHUNKS[c], self.columns), F32)
        (self.kept[c],) = product(
            (0,), None, [acc], self.ids, self.mine[c], self.other[c], self.train, "keep", after
        )
        return self.kept[c]

    def near(self, c, after):
        rows, columns = CHUNKS[c], self.columns
        up, down = call(
            near_kernel, [jax.ShapeDtypeStruct((4, rows, columns), BF16)] * 2,
            [SM] + [VM] * 2, [VM] * 2, [],
            rows * columns, 20 * rows * columns, "near",
        )(after, self.ids, self.acc[c], self.got[c])
        self.up[c] = lax.ppermute(up, "mod", to_y(1))
        self.down[c] = lax.ppermute(down, "mod", to_y(-1))
        return up

    def own(self, group, after):
        members, columns = GROUPS[group], self.columns
        rows = sum(CHUNKS[c] for c in members)
        ins = [a[c] for c in members for a in (self.kept, self.up, self.down)]
        one = jax.ShapeDtypeStruct((rows, columns), BF16)
        stays = jax.ShapeDtypeStruct((rows, columns), F32)
        own, h1, h2, h3 = call(
            functools.partial(own_kernel, len(members)), [stays] + [one] * 3,
            [SM] + [VM] * len(ins), [VM] * 4, [],
            8 * rows * columns, 40 * rows * columns, "own",
        )(after, self.ids, *ins)
        send = functools.partial(lax.ppermute, axis_name="mod")
        h2 = send(h2, perm=to_h(2))
        self.parts[group] = [own, h2, send(h1, perm=to_h(1)), send(h3, perm=to_h(3))]
        return own

    def total(self, group, after):
        at = sum(CHUNKS[:GROUPS[group][0]])
        parts = self.parts[group]
        rows, columns = parts[0].shape
        before = [] if self.out is None else [self.out]
        self.out = call(
            functools.partial(total_kernel, at),
            jax.ShapeDtypeStruct((self.test.shape[1], columns), F32),
            [VM] * 4 + [ANY] * len(before), ANY,
            [pltpu.VMEM((rows, columns), F32), pltpu.SemaphoreType.DMA],
            4 * rows * columns, 16 * rows * columns, "total", {4: 0} if before else {},
        )(after, *parts, *before)
        return parts[0]


def body(train_grads, test_grads, left_inv, right_inv):
    ex = lax.axis_index("ex")
    mod = lax.axis_index("mod")
    ids = jnp.stack([ex // 8, (ex // 2) % 4, ex % 2, mod % 4, mod // 4]).astype(jnp.int32)
    steps = Steps(ids, train_grads, test_grads, (left_inv, right_inv))
    after = []
    for name, which in ORDER:
        done = getattr(steps, name)(which, after)
        after = after if done is None else [done]
    return steps.out


def solution(mesh):
    return jax.shard_map(
        body,
        mesh=mesh,
        in_specs=(
            P("mod", "ex", None),
            P("mod", "ex", None),
            P("mod", None, None),
            P("mod", None, None),
        ),
        out_specs=P("mod", "ex"),
        check_vma=False,
    )
```
